256 devices in a mesh: dom: 16 (over z, core), hour: 16 (over y, x).
Axes of the slice: x: 4, y: 4, z: 8, core: 2. Of those that a mesh axis runs over, the one named last changes fastest.
Arguments:
- inc_local: float32 [16384, 2048], P('dom'), may hold values from -0.125 to 0.125
- inc_bound: float32 [8192, 2048], P('dom'), may hold values from -0.125 to 0.125
- bound_rows: int32 [16, 16, 32], P('dom'), may hold values from 0 to 1023
- bound_count: int32 [16, 16], replicated, may hold values from 0 to 32, as said below
- block_presence_mask: int32 [64, 8], P('dom'), may hold values 0 or 1
- stor_nodes: int32 [16, 128], P('dom'), may hold values from 0 to 1023
- flow0: float32 [32768, 2048], P('dom', 'hour'), may hold values from 0 to 1
- stor0: float32 [2048, 2048], P('dom', 'hour'), may hold values from 0 to 2
- dual0: float32 [16384, 2048], P('dom', 'hour'), may hold values from -6 to 6
- demand: float32 [16384, 2048], P('dom', 'hour'), may hold values from -6 to 6
- pipe_cost: float32 [32768], P('dom'), may hold values from 0.3 to 3
- pipe_cap: float32 [32768], P('dom'), may hold values from 0.5 to 2
- stor_cost: float32 [2048], P('dom'), may hold values from 0.3 to 3
- stor_cap: float32 [2048], P('dom'), may hold values from 1 to 4
Outputs:
- flow: float32 [32768, 2048], P('dom', 'hour')
- level: float32 [2048, 2048], P('dom', 'hour')
- dual: float32 [16384, 2048], P('dom', 'hour')
The draws below stay inside these ranges and needn't reach their ends.
Inputs may be any that keep to these rules, and one draw needn't show every extreme that they name: bound_count[o][q] is 0 where o = q; every owner o has one peer with exactly 32 live slots.
All inputs are finite; a program needn't handle non-finite values. No bound on the sum of `block_presence_mask` on one device may be relied on, other than what follows from the above.
Results may differ from the reference program's by a relative error of at most 0.0001.
Values sent between devices are 32-bit elements; how exact they have to be, the bound alone decides.
A program may use at most 128 MiB of HBM per device.

```python
import math
import jax
import jax.numpy as jnp
from jax import lax

NODE_BLOCKS = 4
PIPE_BLOCKS = 8
CAP = 32
STORE = 128
ITERS = 2
NODE_DEV = 1024
PIPE_DEV = 2048
NODES = 16384
PIPES = 32768
HOURS = 2048
N_DOM = 16


def draw_bound_count(key, part):
    key = jax.random.fold_in(key, 5)
    first, second = jax.random.split(key)
    counts = jax.random.randint(first, (N_DOM, N_DOM), 1, CAP + 1)
    offsets = jax.random.randint(second, (N_DOM,), 1, N_DOM)
    owners = jnp.arange(N_DOM)
    busiest = (owners + offsets) % N_DOM
    counts = jnp.where(owners[None, :] == busiest[:, None], CAP, counts)
    counts = jnp.where(owners[None, :] == owners[:, None], 0, counts)
    return counts.astype(jnp.int32)


def plant(result, rng, least, top_value):
    extent = result.shape
    place = [jax.random.randint(jax.random.fold_in(rng, axis), (), 0, extent[axis]) for axis in range(len(extent))]
    result = result.at[tuple(place)].set(least)
    longest = extent.index(max(extent))
    place[longest] = (place[longest] + 1) % extent[longest]
    return result.at[tuple(place)].set(top_value)


def block_scale(key, extent, cuts, low, top_value):
    def one(position, shards_of):
        heights = jax.random.uniform(jax.random.fold_in(jax.random.fold_in(key, 6), position), (shards_of,), jnp.float32, low / len(cuts), top_value / len(cuts))
        return jnp.repeat(jnp.exp(heights), extent[position] // shards_of).reshape((-1,) + (1,) * (len(extent) - position - 1))

    factor_of = one(*cuts[0])
    for cut in cuts[1:]:
        factor_of = factor_of * one(*cut)
    return factor_of


def noise(rng, extent, spread, limit, cuts=(), dtype=jnp.bfloat16):
    values = spread * jax.random.normal(rng, extent, jnp.float32)
    if cuts:
        values = values * block_scale(rng, extent, cuts, -0.22, 0.18)
    return jnp.clip(values, -limit, limit).astype(dtype)


def setup_inputs(seed: int = 0) -> dict:
    seeds = jax.random.split(jax.random.key(seed), 15)
    return {
        "inc_local": noise(seeds[0], (NODES, PIPE_DEV), PIPE_DEV ** -0.5, 0.125, ((0, 16),), jnp.float32),
        "inc_bound": noise(seeds[1], (N_DOM * N_DOM * CAP, PIPE_DEV), PIPE_DEV ** -0.5, 0.125, ((0, 16),), jnp.float32),
        "bound_rows": plant(jax.random.randint(seeds[2], (N_DOM, N_DOM, CAP), 0, NODE_DEV), jax.random.fold_in(seeds[2], 1), 0, NODE_DEV - 1).astype(jnp.int32),
        "bound_count": draw_bound_count(jax.random.fold_in(seeds[14], 71), 0),
        "block_presence_mask": plant((jax.random.randint(seeds[4], (N_DOM * NODE_BLOCKS, PIPE_BLOCKS), 0, 4) < 3).astype(jnp.int32), jax.random.fold_in(seeds[4], 1), 0, 1),
        "stor_nodes": plant(jax.random.randint(seeds[5], (N_DOM, STORE), 0, NODE_DEV), jax.random.fold_in(seeds[5], 1), 0, NODE_DEV - 1).astype(jnp.int32),
        "flow0": jnp.clip(1.0 * jax.random.uniform(seeds[6], (PIPES, HOURS), jnp.float32) ** block_scale(seeds[6], (PIPES, HOURS), ((0, 16), (1, 16)), -0.2, 0.2), 0.0, 1.0),
        "stor0": jnp.clip(2.0 * jax.random.uniform(seeds[7], (N_DOM * STORE, HOURS), jnp.float32) ** block_scale(seeds[7], (N_DOM * STORE, HOURS), ((0, 16), (1, 16)), -0.2, 0.2), 0.0, 2.0),
        "dual0": noise(seeds[8], (NODES, HOURS), 1.0, 6.0, ((0, 16), (1, 16)), jnp.float32),
        "demand": noise(seeds[9], (NODES, HOURS), 1.0, 6.0, ((0, 16), (1, 16)), jnp.float32),
        "pipe_cost": jnp.clip(jnp.exp(math.log(3.0) - 2.3025851 * jax.random.uniform(seeds[10], (PIPES,), jnp.float32) ** block_scale(seeds[10], (PIPES,), ((0, 16),), -0.2, 0.2)), 0.3, 3.0),
        "pipe_cap": jnp.clip(jnp.exp(math.log(2.0) - 1.3862944 * jax.random.uniform(seeds[11], (PIPES,), jnp.float32) ** block_scale(seeds[11], (PIPES,), ((0, 16),), -0.2, 0.2)), 0.5, 2.0),
        "stor_cost": jnp.clip(jnp.exp(math.log(3.0) - 2.3025851 * jax.random.uniform(seeds[12], (N_DOM * STORE,), jnp.float32) ** block_scale(seeds[12], (N_DOM * STORE,), ((0, 16),), -0.2, 0.2)), 0.3, 3.0),
        "stor_cap": jnp.clip(jnp.exp(math.log(4.0) - 1.3862944 * jax.random.uniform(seeds[13], (N_DOM * STORE,), jnp.float32) ** block_scale(seeds[13], (N_DOM * STORE,), ((0, 16),), -0.2, 0.2)), 1.0, 4.0),
    }


HIGH = lax.Precision.HIGHEST


def reference(inc_local, inc_bound, bound_rows, bound_count, block_presence_mask, stor_nodes, flow0, stor0, dual0, demand, pipe_cost, pipe_cap, stor_cost, stor_cap):
    domain_count = bound_count.shape[0]
    node_per_device = inc_local.shape[0] // domain_count
    pipe_dev = inc_local.shape[1]
    nbn = block_presence_mask.shape[0] // domain_count
    nbp = block_presence_mask.shape[1]
    bsize = node_per_device // nbn
    slots = bound_rows.shape[2]
    hour_steps = flow0.shape[1]
    store = stor_nodes.shape[1]
    local_mat = inc_local.reshape(domain_count, nbn, bsize, nbp, bsize) * block_presence_mask.reshape(domain_count, nbn, 1, nbp, 1).astype(jnp.float32)
    local_mat = local_mat.reshape(domain_count, node_per_device, pipe_dev)
    live = (jnp.arange(slots)[None, None, :] < bound_count.T[:, :, None]).astype(jnp.float32)
    bound_mat = inc_bound.reshape(domain_count, domain_count * slots, pipe_dev) * live.reshape(domain_count, domain_count * slots, 1)
    owners = jnp.arange(domain_count)[:, None, None]
    parts = jnp.arange(domain_count)[:, None]
    f = flow0.reshape(domain_count, pipe_dev, hour_steps)
    s = stor0.reshape(domain_count, store, hour_steps)
    dual_vector = dual0.reshape(domain_count, node_per_device, hour_steps)
    heat_demand = demand.reshape(domain_count, node_per_device, hour_steps)
    pcost = pipe_cost.reshape(domain_count, pipe_dev, 1)
    pcap = pipe_cap.reshape(domain_count, pipe_dev, 1)
    scost = stor_cost.reshape(domain_count, store, 1)
    scap = stor_cap.reshape(domain_count, store, 1)
    for step in range(ITERS):
        bvals = dual_vector[owners, bound_rows]
        bvals = jnp.transpose(bvals, (1, 0, 2, 3)).reshape(domain_count, domain_count * slots, hour_steps)
        grad_f = jnp.einsum("dnp,dnh->dph", local_mat, dual_vector, precision=HIGH) + jnp.einsum("dsp,dsh->dph", bound_mat, bvals, precision=HIGH)
        storage_duals = dual_vector[parts, stor_nodes]
        grad_s = jnp.roll(storage_duals, -1, axis=2) - storage_duals
        f_new = jnp.clip(f - 0.3 * (pcost - grad_f), 0.0, pcap)
        s_new = jnp.clip(s - 0.3 * (scost - grad_s), 0.0, scap)
        fbar = 2.0 * f_new - f
        sbar = 2.0 * s_new - s
        primal_residual = jnp.einsum("dnp,dph->dnh", local_mat, fbar, precision=HIGH)
        terms = jnp.einsum("dsp,dph->dsh", bound_mat, fbar, precision=HIGH).reshape(domain_count, domain_count, slots, hour_steps)
        terms = jnp.transpose(terms, (1, 0, 2, 3))
        primal_residual = primal_residual.at[owners, bound_rows].add(terms)
        primal_residual = primal_residual.at[parts, stor_nodes].add(jnp.roll(sbar, 1, axis=2) - sbar)
        dual_vector = dual_vector + 0.3 * (heat_demand - primal_residual)
        f = f_new
        s = s_new
    return f.reshape(domain_count * pipe_dev, hour_steps), s.reshape(domain_count * store, hour_steps), dual_vector.reshape(domain_count * node_per_device, hour_steps)
```

```python
import jax
import jax.numpy as jnp
from jax import lax
from jax.experimental import pallas as pl
from jax.experimental.pallas import tpu as pltpu
from jax.sharding import PartitionSpec as P

ITERS = 2
STEP = 0.3
HALVES = 2
MESH = pl.DeviceIdType.MESH
F32 = jnp.float32
BF16 = jnp.bfloat16
NN = (((1,), (0,)), ((), ()))
NT = (((1,), (1,)), ((), ()))

GROUPS = (
    ((4, 0), (4, 1), (3, 0), (3, 1), (-3, 0), (-3, 1), (0, 1), (0, 0)),
    ((2, 0), (2, 1), (-2, 0), (-2, 1), (1, 0), (1, 1), (-1, 0), (-1, 1)),
)
BLOCKS = GROUPS[0] + GROUPS[1]
PER = len(GROUPS[0])
OWN = BLOCKS.index((0, 0))
MIRROR = [BLOCKS.index((4 if dz == 4 else -dz, flip)) for dz, flip in BLOCKS]


def dot(a, b, dims):
    return lax.dot_general(a, b, dims, preferred_element_type=F32)


def parts(x):
    hi = x.astype(BF16)
    lo = (x - hi.astype(F32)).astype(BF16)
    return hi, lo


def product(hi, lo, mat_hi, mat_lo, dims):
    n = hi.shape[0]
    both = dot(jnp.concatenate([hi, lo], axis=0), mat_hi, dims)
    return both[:n] + both[n:] + dot(hi, mat_lo, dims)


def exact(hi, lo, onehot, dims):
    n = hi.shape[0]
    both = dot(jnp.concatenate([hi, lo], axis=0), onehot, dims)
    return both[:n] + both[n:]


def swap_blocks(blocks, slots):
    count = len(blocks)
    group = lax.broadcasted_iota(jnp.int32, blocks[0].shape, 1) // slots
    result = []
    for i in range(count):
        out = blocks[i]
        for j in range(count):
            if j != i:
                out = jnp.where(group == j, pltpu.roll(blocks[j], ((j - i) % count) * slots, 1), out)
        result.append(out)
    return result


def kernel(
    inc_local, inc_bound, bound_rows, bound_count, presence, stor_nodes,
    flow0, stor0, dual0, demand, pipe_cost, pipe_cap, stor_cost, stor_cap,
    flow_out, level_out, dual_out,
    loc32, bnd32, loc_hi, loc_lo, bnd_hi, bnd_lo,
    nat_f, nat_y, nat_d, nat_s, rows_v, stor_v, cost_v, cap_v, scost_v, scap_v, count_s, pres_s,
    f_t, y_t, d_t, s_t, g_t, fb, yb, sd, onehot, live, w_t,
    send, recv, halo_send, halo_recv,
    in_sem, loc_sem, bnd_sem, out_sem, send_sem, recv_sem, halo_send_sem, halo_recv_sem,
):
    me = lax.axis_index("dom")
    hour = lax.axis_index("hour")
    hours = lax.axis_size("hour")
    nodes, pipes = inc_local.shape
    slots = bound_rows.shape[1]
    store = stor_nodes.shape[1]
    width = flow0.shape[1]
    half = width // HALVES
    msg = half * slots // 128
    per_tile = 128 // slots
    cols = PER * slots
    all_slots = 2 * cols

    def dom_at(dz, flip):
        z, core = me // 2, lax.rem(me, 2)
        z = lax.rem(z + (dz + 8), 8)
        return z * 2 + (1 - core if flip else core)

    nxt = lax.rem(hour + 1, hours)
    prv = lax.rem(hour + hours - 1, hours)

    barrier = pltpu.get_barrier_semaphore()
    for j, (dz, flip) in enumerate(BLOCKS):
        if j != OWN:
            pl.semaphore_signal(barrier, inc=1, device_id={"dom": dom_at(dz, flip)}, device_id_type=MESH)
    pl.semaphore_signal(barrier, inc=1, device_id={"hour": nxt}, device_id_type=MESH)
    pl.semaphore_signal(barrier, inc=1, device_id={"hour": prv}, device_id_type=MESH)

    ins = [
        (dual0, nat_y), (bound_rows, rows_v), (stor_nodes, stor_v), (bound_count, count_s), (presence, pres_s),
        (pipe_cost, cost_v), (pipe_cap, cap_v), (stor_cost, scost_v), (stor_cap, scap_v), (stor0, nat_s),
        (flow0, nat_f), (demand, nat_d),
    ]
    in_copies = [pltpu.make_async_copy(a, b, in_sem.at[i]) for i, (a, b) in enumerate(ins)]
    (cp_y, cp_rows, cp_stor, cp_count, cp_pres, cp_cost, cp_cap, cp_scost, cp_scap, cp_s, cp_f, cp_d) = in_copies
    n_loc = loc_sem.shape[0]
    n_bnd = bnd_sem.shape[0]
    step_loc = nodes // n_loc
    step_bnd = inc_bound.shape[0] // n_bnd

    def loc_copy(i):
        s = pl.ds(pl.multiple_of(i * step_loc, step_loc), step_loc)
        return pltpu.make_async_copy(inc_local.at[s], loc32.at[s], loc_sem.at[i])

    def bnd_copy(i):
        s = pl.ds(pl.multiple_of(i * step_bnd, step_bnd), step_bnd)
        return pltpu.make_async_copy(inc_bound.at[s], bnd32.at[s], bnd_sem.at[i])

    for c in in_copies[:10]:
        c.start()
    for i in range(n_loc):
        loc_copy(i).start()
    cp_f.start()
    for i in range(n_bnd):
        bnd_copy(i).start()
    cp_d.start()

    zero = jnp.zeros((msg, 128), F32)
    for x in range(2 * ITERS):
        for h in range(HALVES):
            recv[x, h, OWN * msg : (OWN + 1) * msg, :] = zero

    cp_rows.wait()
    cp_stor.wait()
    node = lax.broadcasted_iota(jnp.int32, (nodes, 128), 0)
    for t in range(all_slots // 128):
        pieces = [rows_v[pl.ds(dom_at(*BLOCKS[t * per_tile + p]), 1), :] for p in range(per_tile)]
        row = jnp.concatenate(pieces, axis=1)
        onehot[:, t * 128 : (t + 1) * 128] = jnp.where(node == row, 1.0, 0.0).astype(BF16)
    onehot[:, all_slots:] = jnp.where(node == stor_v[...], 1.0, 0.0).astype(BF16)

    cp_count.wait()
    lane = lax.broadcasted_iota(jnp.int32, (8, 128), 1)
    for t in range(all_slots // 128):
        counts = jnp.zeros((8, 128), jnp.int32)
        for p in range(per_tile):
            counts = jnp.where(lane // slots == p, count_s[dom_at(*BLOCKS[t * per_tile + p]), me], counts)
        live[:, t * 128 : (t + 1) * 128] = jnp.where(lax.rem(lane, slots) < counts, 1.0, 0.0).astype(F32)

    cp_y.wait()
    for j in range(nodes // 128):
        s = slice(j * 128, (j + 1) * 128)
        y_t[:, s] = nat_y[s, :].T
    hi, lo = parts(y_t[...])
    yb[:width, :] = hi
    yb[width:, :] = lo

    def rows_of(h):
        return pl.ds(pl.multiple_of(h * half, half), half)

    def lows_of(h):
        return pl.ds(pl.multiple_of(width + h * half, half), half)

    def message(x, h, j):
        dz, flip = BLOCKS[j]
        k = MIRROR[j]
        return pltpu.make_async_remote_copy(
            src_ref=send.at[x, h, pl.ds(j * msg, msg)],
            dst_ref=recv.at[x, h, pl.ds(k * msg, msg)],
            send_sem=send_sem.at[x, h, j // PER],
            recv_sem=recv_sem.at[x, h, k // PER],
            device_id={"dom": dom_at(dz, flip)},
            device_id_type=MESH,
        )

    def whole(x, h, group):
        count = PER - 1 if OWN // PER == group else PER
        s = pl.ds(group * PER * msg, count * msg)
        return pltpu.make_async_remote_copy(
            src_ref=send.at[x, h, s],
            dst_ref=recv.at[x, h, s],
            send_sem=send_sem.at[x, h, group],
            recv_sem=recv_sem.at[x, h, group],
            device_id={"dom": dom_at(0, 1)},
            device_id_type=MESH,
        )

    def post(x, h, group, values):
        for t in range(cols // 128):
            blocks = [values[g * msg : (g + 1) * msg, t * 128 : (t + 1) * 128] for g in range(per_tile)]
            for p, out in enumerate(swap_blocks(blocks, slots)):
                j = group * PER + t * per_tile + p
                if j != OWN:
                    send[x, h, j * msg : (j + 1) * msg, :] = out
        for j in range(group * PER, (group + 1) * PER):
            if j != OWN:
                message(x, h, j).start()

    def fetch(x, h, group):
        whole(x, h, group).wait_recv()
        columns = []
        for t in range(cols // 128):
            first = group * PER + t * per_tile
            blocks = [recv[x, h, (first + p) * msg : (first + p + 1) * msg, :] for p in range(per_tile)]
            columns.append(jnp.concatenate(swap_blocks(blocks, slots), axis=0))
        return jnp.concatenate(columns, axis=1)

    def gather(it, h):
        for group in range(2):
            s = slice(group * cols, (group + 1) * cols)
            post(2 * it, h, group, exact(yb[rows_of(h), :], yb[lows_of(h), :], onehot[:, s], NN))

    def scatter(it, h):
        total = None
        for group in range(2):
            s = slice(group * cols, (group + 1) * cols)
            hi, lo = parts(fetch(2 * it + 1, h, group))
            term = exact(hi, lo, onehot[:, s], NT)
            total = term if total is None else total + term
        y = y_t[rows_of(h), :] - STEP * total
        y_t[rows_of(h), :] = y
        hi, lo = parts(y)
        yb[rows_of(h), :] = hi
        yb[lows_of(h), :] = lo

    def primal(it, h):
        r = rows_of(h)
        for group in range(2):
            s = slice(group * cols, (group + 1) * cols)
            hi, lo = parts(fetch(2 * it, h, group) * live[0:1, s])
            g_t[r, :] += product(hi, lo, bnd_hi[s, :], bnd_lo[s, :], NN)
        f = f_t[r, :]
        new = jnp.clip(f - STEP * (cost_v[...] - g_t[r, :]), 0.0, cap_v[...])
        f_t[r, :] = new
        hi, lo = parts(2.0 * new - f)
        fb[r, :] = hi
        fb[lows_of(h), :] = lo
        for group in range(2):
            s = slice(group * cols, (group + 1) * cols)
            terms = product(fb[r, :], fb[lows_of(h), :], bnd_hi[s, :], bnd_lo[s, :], NT)
            post(2 * it + 1, h, group, terms * live[0:1, s])

    def halo(it, kind):
        return pltpu.make_async_remote_copy(
            src_ref=halo_send.at[it, kind],
            dst_ref=halo_recv.at[it, kind],
            send_sem=halo_send_sem.at[it, kind],
            recv_sem=halo_recv_sem.at[it, kind],
            device_id={"hour": nxt if kind else prv},
            device_id_type=MESH,
        )

    def prepare():
        cp_pres.wait()
        rows = 64
        bsize = pipes // presence.shape[1]

        def one_loc(i, _):
            @pl.when(lax.rem(i, step_loc // rows) == 0)
            def _():
                loc_copy(i // (step_loc // rows)).wait()

            s = pl.ds(pl.multiple_of(i * rows, rows), rows)
            for j in range(presence.shape[1]):
                c = slice(j * bsize, (j + 1) * bsize)
                scale = pres_s[i // (bsize // rows), j].astype(F32)
                hi, lo = parts(loc32[s, c] * scale)
                loc_hi[s, c] = hi
                loc_lo[s, c] = lo
            return 0

        lax.fori_loop(0, nodes // rows, one_loc, 0)
        g_t[...] = product(yb[:width, :], yb[width:, :], loc_hi[...], loc_lo[...], NN)

    def prepare_rest():
        cp_f.wait()
        for j in range(pipes // 128):
            s = slice(j * 128, (j + 1) * 128)
            f_t[:, s] = nat_f[s, :].T
        for i in range(n_bnd):
            bnd_copy(i).wait()
        for j, (dz, flip) in enumerate(BLOCKS):
            hi, lo = parts(bnd32[pl.ds(pl.multiple_of(dom_at(dz, flip) * slots, slots), slots), :])
            bnd_hi[j * slots : (j + 1) * slots, :] = hi
            bnd_lo[j * slots : (j + 1) * slots, :] = lo
        cp_d.wait()
        for j in range(nodes // 128):
            s = slice(j * 128, (j + 1) * 128)
            d_t[:, s] = nat_d[s, :].T
        cp_s.wait()
        s_t[...] = nat_s[...].T
        cp_cost.wait()
        cp_cap.wait()
        cp_scost.wait()
        cp_scap.wait()

    pl.semaphore_wait(barrier, PER * 2 - 1 + 2)

    row_of = lax.broadcasted_iota(jnp.int32, (width, store), 0)
    stor_cols = slice(all_slots, all_slots + store)

    def iteration(it, _):
        gather(it, 0)

        @pl.when(it > 0)
        def _():
            scatter(it - 1, 1)

        gather(it, 1)
        sd[...] = exact(yb[:width, :], yb[width:, :], onehot[:, stor_cols], NN)
        halo_send[it, 0] = sd[0:8, :]
        halo(it, 0).start()

        @pl.when(it == 0)
        def _():
            prepare()
            prepare_rest()

        @pl.when(it > 0)
        def _():
            g_t[...] = product(yb[:width, :], yb[width:, :], loc_hi[...], loc_lo[...], NN)

        halo(it, 0).wait_recv()
        now = sd[...]
        after = jnp.where(row_of == width - 1, halo_recv[it, 0, 0:1, :], pltpu.roll(now, width - 1, 0))
        s = s_t[...]
        new = jnp.clip(s - STEP * (scost_v[...] - (after - now)), 0.0, scap_v[...])
        s_t[...] = new
        bar = 2.0 * new - s
        w_t[...] = bar
        halo_send[it, 1] = bar[width - 8 :, :]
        halo(it, 1).start()

        primal(it, 0)
        primal(it, 1)

        halo(it, 1).wait_recv()
        bar = w_t[...]
        before = jnp.where(row_of == 0, halo_recv[it, 1, 7:8, :], pltpu.roll(bar, 1, 0))
        hi, lo = parts(before - bar)
        r = exact(hi, lo, onehot[:, stor_cols], NT)
        r = r + product(fb[:width, :], fb[width:, :], loc_hi[...], loc_lo[...], NT)
        y_t[...] = y_t[...] + STEP * (d_t[...] - r)
        scatter(it, 0)
        return 0

    lax.fori_loop(0, ITERS, iteration, 0)
    for j in range(pipes // 128):
        s = slice(j * 128, (j + 1) * 128)
        nat_f[s, :] = f_t[:, s].T
    nat_s[...] = s_t[...].T
    out_f = pltpu.make_async_copy(nat_f, flow_out, out_sem.at[0])
    out_f.start()
    out_s = pltpu.make_async_copy(nat_s, level_out, out_sem.at[1])
    out_s.start()
    scatter(ITERS - 1, 1)
    for j in range(nodes // 128):
        s = slice(j * 128, (j + 1) * 128)
        nat_y[s, :] = y_t[:, s].T
    out_y = pltpu.make_async_copy(nat_y, dual_out, out_sem.at[2])
    out_y.start()
    for x in range(2 * ITERS):
        for h in range(HALVES):
            for group in range(2):
                whole(x, h, group).wait_send()
    for it in range(ITERS):
        for kind in range(2):
            halo(it, kind).wait_send()
    out_f.wait()
    out_s.wait()
    out_y.wait()


def body(
    inc_local, inc_bound, bound_rows, bound_count, block_presence_mask, stor_nodes,
    flow0, stor0, dual0, demand, pipe_cost, pipe_cap, stor_cost, stor_cap,
):
    nodes, pipes = inc_local.shape
    store, width = stor0.shape
    peers, slots = bound_rows.shape[1:]
    all_slots = peers * slots
    half = width // HALVES
    n_msg = 2 * ITERS
    any_spec = pl.BlockSpec(memory_space=pl.ANY)
    vmem = pltpu.VMEM
    sem = pltpu.SemaphoreType.DMA
    args = (
        inc_local, inc_bound, bound_rows[0], bound_count, block_presence_mask, stor_nodes,
        flow0, stor0, dual0, demand, pipe_cost[None], pipe_cap[None], stor_cost[None], stor_cap[None],
    )
    return pl.pallas_call(
        kernel,
        out_shape=(
            jax.ShapeDtypeStruct((pipes, width), F32),
            jax.ShapeDtypeStruct((store, width), F32),
            jax.ShapeDtypeStruct((nodes, width), F32),
        ),
        in_specs=[any_spec] * len(args),
        out_specs=(any_spec,) * 3,
        scratch_shapes=[
            vmem((nodes, pipes), F32),
            vmem((all_slots, pipes), F32),
            vmem((nodes, pipes), BF16),
            vmem((nodes, pipes), BF16),
            vmem((all_slots, pipes), BF16),
            vmem((all_slots, pipes), BF16),
            vmem((pipes, width), F32),
            vmem((nodes, width), F32),
            vmem((nodes, width), F32),
            vmem((store, width), F32),
            vmem((peers, slots), jnp.int32),
            vmem((1, store), jnp.int32),
            vmem((1, pipes), F32),
            vmem((1, pipes), F32),
            vmem((1, store), F32),
            vmem((1, store), F32),
            pltpu.SMEM(bound_count.shape, jnp.int32),
            pltpu.SMEM(block_presence_mask.shape, jnp.int32),
            vmem((width, pipes), F32),
            vmem((width, nodes), F32),
            vmem((width, nodes), F32),
            vmem((width, store), F32),
            vmem((width, pipes), F32),
            vmem((2 * width, pipes), BF16),
            vmem((2 * width, nodes), BF16),
            vmem((width, store), F32),
            vmem((nodes, all_slots + store), BF16),
            vmem((8, all_slots), F32),
            vmem((width, store), F32),
            vmem((n_msg, HALVES, half * all_slots // 128, 128), F32),
            vmem((n_msg, HALVES, half * all_slots // 128, 128), F32),
            vmem((ITERS, 2, 8, store), F32),
            vmem((ITERS, 2, 8, store), F32),
            sem((12,)),
            sem((8,)),
            sem((4,)),
            sem((3,)),
            sem((n_msg, HALVES, 2)),
            sem((n_msg, HALVES, 2)),
            sem((ITERS, 2)),
            sem((ITERS, 2)),
        ],
        compiler_params=pltpu.CompilerParams(
            collective_id=0, has_side_effects=True, vmem_limit_bytes=56 * 2**20
        ),
    )(*args)


def solution(mesh):
    placed = (
        P("dom", None),
        P("dom", None),
        P("dom", None, None),
        P(),
        P("dom", None),
        P("dom", None),
        P("dom", "hour"),
        P("dom", "hour"),
        P("dom", "hour"),
        P("dom", "hour"),
        P("dom"),
        P("dom"),
        P("dom"),
        P("dom"),
    )
    return jax.shard_map(
        body,
        mesh=mesh,
        in_specs=placed,
        out_specs=(P("dom", "hour"), P("dom", "hour"), P("dom", "hour")),
        check_vma=False,
    )
```

```python
import jax
import jax.numpy as jnp
from jax import lax
from jax.experimental import pallas as pl
from jax.experimental.pallas import tpu as pltpu
from jax.sharding import PartitionSpec as P

ITERS = 2
STEP = 0.3
HALVES = 2
MESH = pl.DeviceIdType.MESH
F32 = jnp.float32
BF16 = jnp.bfloat16
NN = (((1,), (0,)), ((), ()))
NT = (((1,), (1,)), ((), ()))

GROUPS = (
    ((4, 0), (4, 1), (3, 0), (3, 1), (-3, 0), (-3, 1), (0, 1), (0, 0)),
    ((2, 0), (2, 1), (-2, 0), (-2, 1), (1, 0), (1, 1), (-1, 0), (-1, 1)),
)
BLOCKS = GROUPS[0] + GROUPS[1]
PER = len(GROUPS[0])
OWN = BLOCKS.index((0, 0))
MIRROR = [BLOCKS.index((4 if dz == 4 else -dz, flip)) for dz, flip in BLOCKS]


def dot(a, b, dims):
    return lax.dot_general(a, b, dims, preferred_element_type=F32)


def parts(x):
    hi = x.astype(BF16)
    lo = (x - hi.astype(F32)).astype(BF16)
    return hi, lo


def product(hi, lo, mat_hi, mat_lo, dims):
    n = hi.shape[0]
    both = dot(jnp.concatenate([hi, lo], axis=0), mat_hi, dims)
    return both[:n] + both[n:] + dot(hi, mat_lo, dims)


def exact(hi, lo, onehot, dims):
    n = hi.shape[0]
    both = dot(jnp.concatenate([hi, lo], axis=0), onehot, dims)
    return both[:n] + both[n:]


def swap_blocks(blocks, slots):
    count = len(blocks)
    group = lax.broadcasted_iota(jnp.int32, blocks[0].shape, 1) // slots
    result = []
    for i in range(count):
        out = blocks[i]
        for j in range(count):
            if j != i:
                out = jnp.where(group == j, pltpu.roll(blocks[j], ((j - i) % count) * slots, 1), out)
        result.append(out)
    return result


def kernel(
    inc_local, inc_bound, bound_rows, bound_count, presence, stor_nodes,
    flow0, stor0, dual0, demand, pipe_cost, pipe_cap, stor_cost, stor_cap,
    flow_out, level_out, dual_out,
    loc32, bnd32, loc_hi, loc_lo, bnd_hi, bnd_lo, bt_hi, bt_lo,
    nat_f, nat_y, nat_d, nat_s, rows_v, stor_v, cost_v, cap_v, scost_v, scap_v, count_s, pres_s,
    f_t, y_t, d_t, s_t, g_t, fb, yb, sd, onehot, live, w_t,
    send, recv, halo_send, halo_recv,
    in_sem, loc_sem, bnd_sem, out_sem, send_sem, recv_sem, halo_send_sem, halo_recv_sem,
):
    me = lax.axis_index("dom")
    hour = lax.axis_index("hour")
    hours = lax.axis_size("hour")
    nodes, pipes = inc_local.shape
    slots = bound_rows.shape[1]
    store = stor_nodes.shape[1]
    width = flow0.shape[1]
    half = width // HALVES
    msg = half * slots // 128
    per_tile = 128 // slots
    cols = PER * slots
    all_slots = 2 * cols

    def dom_at(dz, flip):
        z, core = me // 2, lax.rem(me, 2)
        z = lax.rem(z + (dz + 8), 8)
        return z * 2 + (1 - core if flip else core)

    nxt = lax.rem(hour + 1, hours)
    prv = lax.rem(hour + hours - 1, hours)

    barrier = pltpu.get_barrier_semaphore()
    for j, (dz, flip) in enumerate(BLOCKS):
        if j != OWN:
            pl.semaphore_signal(barrier, inc=1, device_id={"dom": dom_at(dz, flip)}, device_id_type=MESH)
    pl.semaphore_signal(barrier, inc=1, device_id={"hour": nxt}, device_id_type=MESH)
    pl.semaphore_signal(barrier, inc=1, device_id={"hour": prv}, device_id_type=MESH)

    ins = [
        (dual0, nat_y), (bound_rows, rows_v), (stor_nodes, stor_v), (bound_count, count_s), (presence, pres_s),
        (pipe_cost, cost_v), (pipe_cap, cap_v), (stor_cost, scost_v), (stor_cap, scap_v), (stor0, nat_s),
        (flow0, nat_f), (demand, nat_d),
    ]
    in_copies = [pltpu.make_async_copy(a, b, in_sem.at[i]) for i, (a, b) in enumerate(ins)]
    (cp_y, cp_rows, cp_stor, cp_count, cp_pres, cp_cost, cp_cap, cp_scost, cp_scap, cp_s, cp_f, cp_d) = in_copies
    n_loc = loc_sem.shape[0]
    n_bnd = bnd_sem.shape[0]
    step_loc = nodes // n_loc
    step_bnd = inc_bound.shape[0] // n_bnd

    def loc_copy(i):
        s = pl.ds(pl.multiple_of(i * step_loc, step_loc), step_loc)
        return pltpu.make_async_copy(inc_local.at[s], loc32.at[s], loc_sem.at[i])

    def bnd_copy(i):
        s = pl.ds(pl.multiple_of(i * step_bnd, step_bnd), step_bnd)
        return pltpu.make_async_copy(inc_bound.at[s], bnd32.at[s], bnd_sem.at[i])

    for c in in_copies[:10]:
        c.start()
    for i in range(n_loc):
        loc_copy(i).start()
    cp_f.start()
    for i in range(n_bnd):
        bnd_copy(i).start()
    cp_d.start()

    zero = jnp.zeros((msg, 128), F32)
    for x in range(2 * ITERS):
        for h in range(HALVES):
            recv[x, h, OWN * msg : (OWN + 1) * msg, :] = zero

    cp_rows.wait()
    cp_stor.wait()
    node = lax.broadcasted_iota(jnp.int32, (nodes, 128), 0)
    for t in range(all_slots // 128):
        pieces = [rows_v[pl.ds(dom_at(*BLOCKS[t * per_tile + p]), 1), :] for p in range(per_tile)]
        row = jnp.concatenate(pieces, axis=1)
        onehot[:, t * 128 : (t + 1) * 128] = jnp.where(node == row, 1.0, 0.0).astype(BF16)
    onehot[:, all_slots:] = jnp.where(node == stor_v[...], 1.0, 0.0).astype(BF16)

    cp_count.wait()
    lane = lax.broadcasted_iota(jnp.int32, (8, 128), 1)
    for t in range(all_slots // 128):
        counts = jnp.zeros((8, 128), jnp.int32)
        for p in range(per_tile):
            counts = jnp.where(lane // slots == p, count_s[dom_at(*BLOCKS[t * per_tile + p]), me], counts)
        live[:, t * 128 : (t + 1) * 128] = jnp.where(lax.rem(lane, slots) < counts, 1.0, 0.0).astype(F32)

    cp_y.wait()
    for j in range(nodes // 128):
        s = slice(j * 128, (j + 1) * 128)
        y_t[:, s] = nat_y[s, :].T
    hi, lo = parts(y_t[...])
    yb[:width, :] = hi
    yb[width:, :] = lo

    def rows_of(h):
        return pl.ds(pl.multiple_of(h * half, half), half)

    def lows_of(h):
        return pl.ds(pl.multiple_of(width + h * half, half), half)

    def message(x, h, j):
        dz, flip = BLOCKS[j]
        k = MIRROR[j]
        return pltpu.make_async_remote_copy(
            src_ref=send.at[x, h, pl.ds(j * msg, msg)],
            dst_ref=recv.at[x, h, pl.ds(k * msg, msg)],
            send_sem=send_sem.at[x, h, j // PER],
            recv_sem=recv_sem.at[x, h, k // PER],
            device_id={"dom": dom_at(dz, flip)},
            device_id_type=MESH,
        )

    def whole(x, h, group):
        count = PER - 1 if OWN // PER == group else PER
        s = pl.ds(group * PER * msg, count * msg)
        return pltpu.make_async_remote_copy(
            src_ref=send.at[x, h, s],
            dst_ref=recv.at[x, h, s],
            send_sem=send_sem.at[x, h, group],
            recv_sem=recv_sem.at[x, h, group],
            device_id={"dom": dom_at(0, 1)},
            device_id_type=MESH,
        )

    def post(x, h, group, values):
        for t in range(cols // 128):
            blocks = [values[g * msg : (g + 1) * msg, t * 128 : (t + 1) * 128] for g in range(per_tile)]
            for p, out in enumerate(swap_blocks(blocks, slots)):
                j = group * PER + t * per_tile + p
                if j != OWN:
                    send[x, h, j * msg : (j + 1) * msg, :] = out
        for j in range(group * PER, (group + 1) * PER):
            if j != OWN:
                message(x, h, j).start()

    def fetch(x, h, group):
        whole(x, h, group).wait_recv()
        columns = []
        for t in range(cols // 128):
            first = group * PER + t * per_tile
            blocks = [recv[x, h, (first + p) * msg : (first + p + 1) * msg, :] for p in range(per_tile)]
            columns.append(jnp.concatenate(swap_blocks(blocks, slots), axis=0))
        return jnp.concatenate(columns, axis=1)

    def gather(it, h):
        values = exact(yb[rows_of(h), :], yb[lows_of(h), :], onehot[:, :all_slots], NN)
        for group in range(2):
            post(2 * it, h, group, values[:, group * cols : (group + 1) * cols])

    def scatter(it, h):
        hi, lo = parts(jnp.concatenate([fetch(2 * it + 1, h, group) for group in range(2)], axis=1))
        total = exact(hi, lo, onehot[:, :all_slots], NT)
        y = y_t[rows_of(h), :] - STEP * total
        y_t[rows_of(h), :] = y
        hi, lo = parts(y)
        yb[rows_of(h), :] = hi
        yb[lows_of(h), :] = lo

    def primal(it, h):
        r = rows_of(h)
        for group in range(2):
            s = slice(group * cols, (group + 1) * cols)
            hi, lo = parts(fetch(2 * it, h, group) * live[0:1, s])
            g_t[r, :] += product(hi, lo, bnd_hi[s, :], bnd_lo[s, :], NN)
        f = f_t[r, :]
        new = jnp.clip(f - STEP * (cost_v[...] - g_t[r, :]), 0.0, cap_v[...])
        f_t[r, :] = new
        hi, lo = parts(2.0 * new - f)
        fb[r, :] = hi
        fb[lows_of(h), :] = lo
        terms = product(fb[r, :], fb[lows_of(h), :], bt_hi[...], bt_lo[...], NN) * live[0:1, :]
        for group in range(2):
            s = slice(group * cols, (group + 1) * cols)
            post(2 * it + 1, h, group, terms[:, s])

    def halo(it, kind):
        return pltpu.make_async_remote_copy(
            src_ref=halo_send.at[it, kind],
            dst_ref=halo_recv.at[it, kind],
            send_sem=halo_send_sem.at[it, kind],
            recv_sem=halo_recv_sem.at[it, kind],
            device_id={"hour": nxt if kind else prv},
            device_id_type=MESH,
        )

    def prepare():
        cp_pres.wait()
        rows = 64
        bsize = pipes // presence.shape[1]

        def one_loc(i, _):
            @pl.when(lax.rem(i, step_loc // rows) == 0)
            def _():
                loc_copy(i // (step_loc // rows)).wait()

            s = pl.ds(pl.multiple_of(i * rows, rows), rows)
            for j in range(presence.shape[1]):
                c = slice(j * bsize, (j + 1) * bsize)
                scale = pres_s[i // (bsize // rows), j].astype(F32)
                hi, lo = parts(loc32[s, c] * scale)
                loc_hi[s, c] = hi
                loc_lo[s, c] = lo
            return 0

        lax.fori_loop(0, nodes // rows, one_loc, 0)
        g_t[...] = product(yb[:width, :], yb[width:, :], loc_hi[...], loc_lo[...], NN)

    def prepare_rest():
        cp_f.wait()
        for j in range(pipes // 128):
            s = slice(j * 128, (j + 1) * 128)
            f_t[:, s] = nat_f[s, :].T
        for i in range(n_bnd):
            bnd_copy(i).wait()
        for j, (dz, flip) in enumerate(BLOCKS):
            hi, lo = parts(bnd32[pl.ds(pl.multiple_of(dom_at(dz, flip) * slots, slots), slots), :])
            bnd_hi[j * slots : (j + 1) * slots, :] = hi
            bnd_lo[j * slots : (j + 1) * slots, :] = lo
        bt_hi[...] = bnd_hi[...].T
        bt_lo[...] = bnd_lo[...].T
        cp_d.wait()
        for j in range(nodes // 128):
            s = slice(j * 128, (j + 1) * 128)
            d_t[:, s] = nat_d[s, :].T
        cp_s.wait()
        s_t[...] = nat_s[...].T
        cp_cost.wait()
        cp_cap.wait()
        cp_scost.wait()
        cp_scap.wait()

    pl.semaphore_wait(barrier, PER * 2 - 1 + 2)

    row_of = lax.broadcasted_iota(jnp.int32, (width, store), 0)
    stor_cols = slice(all_slots, all_slots + store)

    def iteration(it, _):
        gather(it, 0)

        @pl.when(it > 0)
        def _():
            scatter(it - 1, 1)

        gather(it, 1)
        sd[...] = exact(yb[:width, :], yb[width:, :], onehot[:, stor_cols], NN)
        halo_send[it, 0] = sd[0:8, :]
        halo(it, 0).start()

        @pl.when(it == 0)
        def _():
            prepare()
            prepare_rest()

        @pl.when(it > 0)
        def _():
            g_t[...] = product(yb[:width, :], yb[width:, :], loc_hi[...], loc_lo[...], NN)

        halo(it, 0).wait_recv()
        now = sd[...]
        after = jnp.where(row_of == width - 1, halo_recv[it, 0, 0:1, :], pltpu.roll(now, width - 1, 0))
        s = s_t[...]
        new = jnp.clip(s - STEP * (scost_v[...] - (after - now)), 0.0, scap_v[...])
        s_t[...] = new
        bar = 2.0 * new - s
        w_t[...] = bar
        halo_send[it, 1] = bar[width - 8 :, :]
        halo(it, 1).start()

        primal(it, 0)
        primal(it, 1)

        halo(it, 1).wait_recv()
        bar = w_t[...]
        before = jnp.where(row_of == 0, halo_recv[it, 1, 7:8, :], pltpu.roll(bar, 1, 0))
        hi, lo = parts(before - bar)
        r = exact(hi, lo, onehot[:, stor_cols], NT)
        r = r + product(fb[:width, :], fb[width:, :], loc_hi[...], loc_lo[...], NT)
        y_t[...] = y_t[...] + STEP * (d_t[...] - r)
        scatter(it, 0)
        return 0

    lax.fori_loop(0, ITERS, iteration, 0)
    for j in range(pipes // 128):
        s = slice(j * 128, (j + 1) * 128)
        nat_f[s, :] = f_t[:, s].T
    nat_s[...] = s_t[...].T
    out_f = pltpu.make_async_copy(nat_f, flow_out, out_sem.at[0])
    out_f.start()
    out_s = pltpu.make_async_copy(nat_s, level_out, out_sem.at[1])
    out_s.start()
    scatter(ITERS - 1, 1)
    for j in range(nodes // 128):
        s = slice(j * 128, (j + 1) * 128)
        nat_y[s, :] = y_t[:, s].T
    out_y = pltpu.make_async_copy(nat_y, dual_out, out_sem.at[2])
    out_y.start()
    for x in range(2 * ITERS):
        for h in range(HALVES):
            for group in range(2):
                whole(x, h, group).wait_send()
    for it in range(ITERS):
        for kind in range(2):
            halo(it, kind).wait_send()
    out_f.wait()
    out_s.wait()
    out_y.wait()


def store_all(flow_in, level_in, dual_in, flow_out, level_out, dual_out, flow, level, dual, sems, in_sems):
    pairs = ((flow, flow_out), (level, level_out), (dual, dual_out))
    copies = [pltpu.make_async_copy(a, b, sems.at[i]) for i, (a, b) in enumerate(pairs)]
    loads = [pltpu.make_async_copy(a, b, in_sems.at[i]) for i, (a, b) in enumerate(((flow_in, flow), (level_in, level), (dual_in, dual)))]
    for c in loads:
        c.start()
    for a, c in zip(loads, copies):
        a.wait()
        c.start()
    for c in copies:
        c.wait()


def body(
    inc_local, inc_bound, bound_rows, bound_count, block_presence_mask, stor_nodes,
    flow0, stor0, dual0, demand, pipe_cost, pipe_cap, stor_cost, stor_cap,
):
    nodes, pipes = inc_local.shape
    store, width = stor0.shape
    peers, slots = bound_rows.shape[1:]
    all_slots = peers * slots
    half = width // HALVES
    n_msg = 2 * ITERS
    any_spec = pl.BlockSpec(memory_space=pl.ANY)
    vmem = pltpu.VMEM
    sem = pltpu.SemaphoreType.DMA
    args = (
        inc_local, inc_bound, bound_rows[0], bound_count, block_presence_mask, stor_nodes,
        flow0, stor0, dual0, demand, pipe_cost[None], pipe_cap[None], stor_cost[None], stor_cap[None],
    )
    results = pl.pallas_call(
        kernel,
        out_shape=(
            jax.ShapeDtypeStruct((pipes, width), F32),
            jax.ShapeDtypeStruct((store, width), F32),
            jax.ShapeDtypeStruct((nodes, width), F32),
        ),
        in_specs=[any_spec] * len(args),
        out_specs=(any_spec,) * 3,
        scratch_shapes=[
            vmem((nodes, pipes), F32),
            vmem((all_slots, pipes), F32),
            vmem((nodes, pipes), BF16),
            vmem((nodes, pipes), BF16),
            vmem((all_slots, pipes), BF16),
            vmem((all_slots, pipes), BF16),
            vmem((pipes, all_slots), BF16),
            vmem((pipes, all_slots), BF16),
            vmem((pipes, width), F32),
            vmem((nodes, width), F32),
            vmem((nodes, width), F32),
            vmem((store, width), F32),
            vmem((peers, slots), jnp.int32),
            vmem((1, store), jnp.int32),
            vmem((1, pipes), F32),
            vmem((1, pipes), F32),
            vmem((1, store), F32),
            vmem((1, store), F32),
            pltpu.SMEM(bound_count.shape, jnp.int32),
            pltpu.SMEM(block_presence_mask.shape, jnp.int32),
            vmem((width, pipes), F32),
            vmem((width, nodes), F32),
            vmem((width, nodes), F32),
            vmem((width, store), F32),
            vmem((width, pipes), F32),
            vmem((2 * width, pipes), BF16),
            vmem((2 * width, nodes), BF16),
            vmem((width, store), F32),
            vmem((nodes, all_slots + store), BF16),
            vmem((8, all_slots), F32),
            vmem((width, store), F32),
            vmem((n_msg, HALVES, half * all_slots // 128, 128), F32),
            vmem((n_msg, HALVES, half * all_slots // 128, 128), F32),
            vmem((ITERS, 2, 8, store), F32),
            vmem((ITERS, 2, 8, store), F32),
            sem((12,)),
            sem((8,)),
            sem((4,)),
            sem((3,)),
            sem((n_msg, HALVES, 2)),
            sem((n_msg, HALVES, 2)),
            sem((ITERS, 2)),
            sem((ITERS, 2)),
        ],
        compiler_params=pltpu.CompilerParams(
            collective_id=0, has_side_effects=True, vmem_limit_bytes=56 * 2**20
        ),
    )(*args)
    return pl.pallas_call(
        store_all,
        out_shape=tuple(jax.ShapeDtypeStruct(r.shape, r.dtype) for r in results),
        in_specs=[any_spec] * 3,
        out_specs=(any_spec,) * 3,
        scratch_shapes=[vmem(r.shape, F32) for r in results] + [sem((3,)), sem((3,))],
    )(*results)


def solution(mesh):
    placed = (
        P("dom", None),
        P("dom", None),
        P("dom", None, None),
        P(),
        P("dom", None),
        P("dom", None),
        P("dom", "hour"),
        P("dom", "hour"),
        P("dom", "hour"),
        P("dom", "hour"),
        P("dom"),
        P("dom"),
        P("dom"),
        P("dom"),
    )
    return jax.shard_map(
        body,
        mesh=mesh,
        in_specs=placed,
        out_specs=(P("dom", "hour"), P("dom", "hour"), P("dom", "hour")),
        check_vma=False,
    )
```

```python
import jax
import jax.numpy as jnp
from jax import lax
from jax.experimental import pallas as pl
from jax.experimental.pallas import tpu as pltpu
from jax.sharding import PartitionSpec as P

ITERS = 2
STEP = 0.3
HALVES = 2
MESH = pl.DeviceIdType.MESH
F32 = jnp.float32
BF16 = jnp.bfloat16
NN = (((1,), (0,)), ((), ()))
NT = (((1,), (1,)), ((), ()))

GROUPS = (
    ((4, 1), (4, 0), (3, 1), (3, 0), (-3, 1), (-3, 0), (0, 1), (0, 0)),
    ((2, 1), (2, 0), (-2, 1), (-2, 0), (1, 1), (1, 0), (-1, 1), (-1, 0)),
)
BLOCKS = GROUPS[0] + GROUPS[1]
PER = len(GROUPS[0])
OWN = BLOCKS.index((0, 0))
MIRROR = [BLOCKS.index((4 if dz == 4 else -dz, flip)) for dz, flip in BLOCKS]


def dot(a, b, dims):
    return lax.dot_general(a, b, dims, preferred_element_type=F32)


def parts(x):
    hi = x.astype(BF16)
    lo = (x - hi.astype(F32)).astype(BF16)
    return hi, lo


def product(hi, lo, mat_hi, mat_lo, dims):
    n = hi.shape[0]
    both = dot(jnp.concatenate([hi, lo], axis=0), mat_hi, dims)
    return both[:n] + both[n:] + dot(hi, mat_lo, dims)


def exact(hi, lo, onehot, dims):
    n = hi.shape[0]
    both = dot(jnp.concatenate([hi, lo], axis=0), onehot, dims)
    return both[:n] + both[n:]


def swap_blocks(blocks, slots):
    count = len(blocks)
    group = lax.broadcasted_iota(jnp.int32, blocks[0].shape, 1) // slots
    result = []
    for i in range(count):
        out = blocks[i]
        for j in range(count):
            if j != i:
                out = jnp.where(group == j, pltpu.roll(blocks[j], ((j - i) % count) * slots, 1), out)
        result.append(out)
    return result


def kernel(
    inc_local, inc_bound, bound_rows, bound_count, presence, stor_nodes,
    flow0, stor0, dual0, demand, pipe_cost, pipe_cap, stor_cost, stor_cap,
    flow_out, level_out, dual_out,
    loc32, bnd32, loc_hi, loc_lo, bnd_hi, bnd_lo, bt_hi, bt_lo,
    nat_f, nat_y, nat_d, nat_s, rows_v, stor_v, cost_v, cap_v, scost_v, scap_v, count_s, pres_s,
    f_t, y_t, d_t, s_t, g_t, fb, yb, sd, onehot, live, w_t,
    send, recv, halo_send, halo_recv,
    in_sem, loc_sem, bnd_sem, out_sem, send_sem, recv_sem, halo_send_sem, halo_recv_sem,
):
    me = lax.axis_index("dom")
    hour = lax.axis_index("hour")
    hours = lax.axis_size("hour")
    nodes, pipes = inc_local.shape
    slots = bound_rows.shape[1]
    store = stor_nodes.shape[1]
    width = flow0.shape[1]
    half = width // HALVES
    msg = half * slots // 128
    per_tile = 128 // slots
    cols = PER * slots
    all_slots = 2 * cols

    def dom_at(dz, flip):
        z, core = me // 2, lax.rem(me, 2)
        z = lax.rem(z + (dz + 8), 8)
        return z * 2 + (1 - core if flip else core)

    nxt = lax.rem(hour + 1, hours)
    prv = lax.rem(hour + hours - 1, hours)

    barrier = pltpu.get_barrier_semaphore()
    for j, (dz, flip) in enumerate(BLOCKS):
        if j != OWN:
            pl.semaphore_signal(barrier, inc=1, device_id={"dom": dom_at(dz, flip)}, device_id_type=MESH)
    pl.semaphore_signal(barrier, inc=1, device_id={"hour": nxt}, device_id_type=MESH)
    pl.semaphore_signal(barrier, inc=1, device_id={"hour": prv}, device_id_type=MESH)

    ins = [
        (dual0, nat_y), (bound_rows, rows_v), (stor_nodes, stor_v), (bound_count, count_s), (presence, pres_s),
        (pipe_cost, cost_v), (pipe_cap, cap_v), (stor_cost, scost_v), (stor_cap, scap_v), (stor0, nat_s),
        (flow0, nat_f), (demand, nat_d),
    ]
    in_copies = [pltpu.make_async_copy(a, b, in_sem.at[i]) for i, (a, b) in enumerate(ins)]
    (cp_y, cp_rows, cp_stor, cp_count, cp_pres, cp_cost, cp_cap, cp_scost, cp_scap, cp_s, cp_f, cp_d) = in_copies
    n_loc = loc_sem.shape[0]
    n_bnd = bnd_sem.shape[0]
    step_loc = nodes // n_loc
    step_bnd = inc_bound.shape[0] // n_bnd

    def loc_copy(i):
        s = pl.ds(pl.multiple_of(i * step_loc, step_loc), step_loc)
        return pltpu.make_async_copy(inc_local.at[s], loc32.at[s], loc_sem.at[i])

    def bnd_copy(i):
        s = pl.ds(pl.multiple_of(i * step_bnd, step_bnd), step_bnd)
        return pltpu.make_async_copy(inc_bound.at[s], bnd32.at[s], bnd_sem.at[i])

    for c in in_copies[:10]:
        c.start()
    for i in range(n_loc):
        loc_copy(i).start()
    cp_f.start()
    for i in range(n_bnd):
        bnd_copy(i).start()
    cp_d.start()

    zero = jnp.zeros((msg, 128), F32)
    for x in range(2 * ITERS):
        for h in range(HALVES):
            recv[x, h, OWN * msg : (OWN + 1) * msg, :] = zero

    cp_rows.wait()
    cp_stor.wait()
    node = lax.broadcasted_iota(jnp.int32, (nodes, 128), 0)
    for t in range(all_slots // 128):
        pieces = [rows_v[pl.ds(dom_at(*BLOCKS[t * per_tile + p]), 1), :] for p in range(per_tile)]
        row = jnp.concatenate(pieces, axis=1)
        onehot[:, t * 128 : (t + 1) * 128] = jnp.where(node == row, 1.0, 0.0).astype(BF16)
    onehot[:, all_slots:] = jnp.where(node == stor_v[...], 1.0, 0.0).astype(BF16)

    cp_count.wait()
    lane = lax.broadcasted_iota(jnp.int32, (8, 128), 1)
    for t in range(all_slots // 128):
        counts = jnp.zeros((8, 128), jnp.int32)
        for p in range(per_tile):
            counts = jnp.where(lane // slots == p, count_s[dom_at(*BLOCKS[t * per_tile + p]), me], counts)
        live[:, t * 128 : (t + 1) * 128] = jnp.where(lax.rem(lane, slots) < counts, 1.0, 0.0).astype(F32)

    cp_y.wait()
    for j in range(nodes // 128):
        s = slice(j * 128, (j + 1) * 128)
        y_t[:, s] = nat_y[s, :].T
    hi, lo = parts(y_t[...])
    yb[:width, :] = hi
    yb[width:, :] = lo

    def rows_of(h):
        return pl.ds(pl.multiple_of(h * half, half), half)

    def lows_of(h):
        return pl.ds(pl.multiple_of(width + h * half, half), half)

    def message(x, h, j):
        dz, flip = BLOCKS[j]
        k = MIRROR[j]
        return pltpu.make_async_remote_copy(
            src_ref=send.at[x, h, pl.ds(j * msg, msg)],
            dst_ref=recv.at[x, h, pl.ds(k * msg, msg)],
            send_sem=send_sem.at[x, h, j // PER],
            recv_sem=recv_sem.at[x, h, k // PER],
            device_id={"dom": dom_at(dz, flip)},
            device_id_type=MESH,
        )

    def whole(x, h, group):
        count = PER - 1 if OWN // PER == group else PER
        s = pl.ds(group * PER * msg, count * msg)
        return pltpu.make_async_remote_copy(
            src_ref=send.at[x, h, s],
            dst_ref=recv.at[x, h, s],
            send_sem=send_sem.at[x, h, group],
            recv_sem=recv_sem.at[x, h, group],
            device_id={"dom": dom_at(0, 1)},
            device_id_type=MESH,
        )

    def post(x, h, group, values):
        for t in range(cols // 128):
            blocks = [values[g * msg : (g + 1) * msg, t * 128 : (t + 1) * 128] for g in range(per_tile)]
            for p, out in enumerate(swap_blocks(blocks, slots)):
                j = group * PER + t * per_tile + p
                if j != OWN:
                    send[x, h, j * msg : (j + 1) * msg, :] = out
        for j in range(group * PER, (group + 1) * PER):
            if j != OWN:
                message(x, h, j).start()

    def fetch(x, h, group):
        whole(x, h, group).wait_recv()
        columns = []
        for t in range(cols // 128):
            first = group * PER + t * per_tile
            blocks = [recv[x, h, (first + p) * msg : (first + p + 1) * msg, :] for p in range(per_tile)]
            columns.append(jnp.concatenate(swap_blocks(blocks, slots), axis=0))
        return jnp.concatenate(columns, axis=1)

    def gather(it, h):
        values = exact(yb[rows_of(h), :], yb[lows_of(h), :], onehot[:, :all_slots], NN)
        for group in range(2):
            post(2 * it, h, group, values[:, group * cols : (group + 1) * cols])

    def scatter(it, h):
        hi, lo = parts(jnp.concatenate([fetch(2 * it + 1, h, group) for group in range(2)], axis=1))
        total = exact(hi, lo, onehot[:, :all_slots], NT)
        y = y_t[rows_of(h), :] - STEP * total
        y_t[rows_of(h), :] = y
        hi, lo = parts(y)
        yb[rows_of(h), :] = hi
        yb[lows_of(h), :] = lo

    def primal(it, h):
        r = rows_of(h)
        for group in range(2):
            s = slice(group * cols, (group + 1) * cols)
            hi, lo = parts(fetch(2 * it, h, group) * live[0:1, s])
            g_t[r, :] += product(hi, lo, bnd_hi[s, :], bnd_lo[s, :], NN)
        f = f_t[r, :]
        new = jnp.clip(f - STEP * (cost_v[...] - g_t[r, :]), 0.0, cap_v[...])
        f_t[r, :] = new
        hi, lo = parts(2.0 * new - f)
        fb[r, :] = hi
        fb[lows_of(h), :] = lo
        terms = product(fb[r, :], fb[lows_of(h), :], bt_hi[...], bt_lo[...], NN) * live[0:1, :]
        for group in range(2):
            s = slice(group * cols, (group + 1) * cols)
            post(2 * it + 1, h, group, terms[:, s])

    def halo(it, kind):
        return pltpu.make_async_remote_copy(
            src_ref=halo_send.at[it, kind],
            dst_ref=halo_recv.at[it, kind],
            send_sem=halo_send_sem.at[it, kind],
            recv_sem=halo_recv_sem.at[it, kind],
            device_id={"hour": nxt if kind else prv},
            device_id_type=MESH,
        )

    def prepare():
        cp_pres.wait()
        rows = 64
        bsize = pipes // presence.shape[1]

        def one_loc(i, _):
            @pl.when(lax.rem(i, step_loc // rows) == 0)
            def _():
                loc_copy(i // (step_loc // rows)).wait()

            s = pl.ds(pl.multiple_of(i * rows, rows), rows)
            for j in range(presence.shape[1]):
                c = slice(j * bsize, (j + 1) * bsize)
                scale = pres_s[i // (bsize // rows), j].astype(F32)
                hi, lo = parts(loc32[s, c] * scale)
                loc_hi[s, c] = hi
                loc_lo[s, c] = lo
            return 0

        lax.fori_loop(0, nodes // rows, one_loc, 0)
        g_t[...] = product(yb[:width, :], yb[width:, :], loc_hi[...], loc_lo[...], NN)

    def prepare_rest():
        cp_f.wait()
        for j in range(pipes // 128):
            s = slice(j * 128, (j + 1) * 128)
            f_t[:, s] = nat_f[s, :].T
        for i in range(n_bnd):
            bnd_copy(i).wait()
        for j, (dz, flip) in enumerate(BLOCKS):
            hi, lo = parts(bnd32[pl.ds(pl.multiple_of(dom_at(dz, flip) * slots, slots), slots), :])
            bnd_hi[j * slots : (j + 1) * slots, :] = hi
            bnd_lo[j * slots : (j + 1) * slots, :] = lo
        bt_hi[...] = bnd_hi[...].T
        bt_lo[...] = bnd_lo[...].T
        cp_d.wait()
        for j in range(nodes // 128):
            s = slice(j * 128, (j + 1) * 128)
            d_t[:, s] = nat_d[s, :].T
        cp_s.wait()
        s_t[...] = nat_s[...].T
        cp_cost.wait()
        cp_cap.wait()
        cp_scost.wait()
        cp_scap.wait()

    pl.semaphore_wait(barrier, PER * 2 - 1 + 2)

    row_of = lax.broadcasted_iota(jnp.int32, (width, store), 0)
    stor_cols = slice(all_slots, all_slots + store)

    def iteration(it, _):
        gather(it, 0)

        @pl.when(it > 0)
        def _():
            scatter(it - 1, 1)

        gather(it, 1)
        sd[...] = exact(yb[:width, :], yb[width:, :], onehot[:, stor_cols], NN)
        halo_send[it, 0] = sd[0:8, :]
        halo(it, 0).start()

        @pl.when(it == 0)
        def _():
            prepare()
            prepare_rest()

        @pl.when(it > 0)
        def _():
            g_t[...] = product(yb[:width, :], yb[width:, :], loc_hi[...], loc_lo[...], NN)

        halo(it, 0).wait_recv()
        now = sd[...]
        after = jnp.where(row_of == width - 1, halo_recv[it, 0, 0:1, :], pltpu.roll(now, width - 1, 0))
        s = s_t[...]
        new = jnp.clip(s - STEP * (scost_v[...] - (after - now)), 0.0, scap_v[...])
        s_t[...] = new
        bar = 2.0 * new - s
        w_t[...] = bar
        halo_send[it, 1] = bar[width - 8 :, :]
        halo(it, 1).start()

        primal(it, 0)
        primal(it, 1)

        halo(it, 1).wait_recv()
        bar = w_t[...]
        before = jnp.where(row_of == 0, halo_recv[it, 1, 7:8, :], pltpu.roll(bar, 1, 0))
        hi, lo = parts(before - bar)
        r = exact(hi, lo, onehot[:, stor_cols], NT)
        r = r + product(fb[:width, :], fb[width:, :], loc_hi[...], loc_lo[...], NT)
        y_t[...] = y_t[...] + STEP * (d_t[...] - r)
        scatter(it, 0)
        return 0

    lax.fori_loop(0, ITERS, iteration, 0)
    for j in range(pipes // 128):
        s = slice(j * 128, (j + 1) * 128)
        nat_f[s, :] = f_t[:, s].T
    nat_s[...] = s_t[...].T
    out_f = pltpu.make_async_copy(nat_f, flow_out, out_sem.at[0])
    out_f.start()
    out_s = pltpu.make_async_copy(nat_s, level_out, out_sem.at[1])
    out_s.start()
    scatter(ITERS - 1, 1)
    for j in range(nodes // 128):
        s = slice(j * 128, (j + 1) * 128)
        nat_y[s, :] = y_t[:, s].T
    out_y = pltpu.make_async_copy(nat_y, dual_out, out_sem.at[2])
    out_y.start()
    for x in range(2 * ITERS):
        for h in range(HALVES):
            for group in range(2):
                whole(x, h, group).wait_send()
    for it in range(ITERS):
        for kind in range(2):
            halo(it, kind).wait_send()
    out_f.wait()
    out_s.wait()
    out_y.wait()


def store_all(flow_in, level_in, dual_in, flow_out, level_out, dual_out, flow, level, dual, sems, in_sems):
    pairs = ((flow, flow_out), (level, level_out), (dual, dual_out))
    copies = [pltpu.make_async_copy(a, b, sems.at[i]) for i, (a, b) in enumerate(pairs)]
    loads = [pltpu.make_async_copy(a, b, in_sems.at[i]) for i, (a, b) in enumerate(((flow_in, flow), (level_in, level), (dual_in, dual)))]
    for c in loads:
        c.start()
    for a, c in zip(loads, copies):
        a.wait()
        c.start()
    for c in copies:
        c.wait()


def body(
    inc_local, inc_bound, bound_rows, bound_count, block_presence_mask, stor_nodes,
    flow0, stor0, dual0, demand, pipe_cost, pipe_cap, stor_cost, stor_cap,
):
    nodes, pipes = inc_local.shape
    store, width = stor0.shape
    peers, slots = bound_rows.shape[1:]
    all_slots = peers * slots
    half = width // HALVES
    n_msg = 2 * ITERS
    any_spec = pl.BlockSpec(memory_space=pl.ANY)
    vmem = pltpu.VMEM
    sem = pltpu.SemaphoreType.DMA
    args = (
        inc_local, inc_bound, bound_rows[0], bound_count, block_presence_mask, stor_nodes,
        flow0, stor0, dual0, demand, pipe_cost[None], pipe_cap[None], stor_cost[None], stor_cap[None],
    )
    results = pl.pallas_call(
        kernel,
        out_shape=(
            jax.ShapeDtypeStruct((pipes, width), F32),
            jax.ShapeDtypeStruct((store, width), F32),
            jax.ShapeDtypeStruct((nodes, width), F32),
        ),
        in_specs=[any_spec] * len(args),
        out_specs=(any_spec,) * 3,
        scratch_shapes=[
            vmem((nodes, pipes), F32),
            vmem((all_slots, pipes), F32),
            vmem((nodes, pipes), BF16),
            vmem((nodes, pipes), BF16),
            vmem((all_slots, pipes), BF16),
            vmem((all_slots, pipes), BF16),
            vmem((pipes, all_slots), BF16),
            vmem((pipes, all_slots), BF16),
            vmem((pipes, width), F32),
            vmem((nodes, width), F32),
            vmem((nodes, width), F32),
            vmem((store, width), F32),
            vmem((peers, slots), jnp.int32),
            vmem((1, store), jnp.int32),
            vmem((1, pipes), F32),
            vmem((1, pipes), F32),
            vmem((1, store), F32),
            vmem((1, store), F32),
            pltpu.SMEM(bound_count.shape, jnp.int32),
            pltpu.SMEM(block_presence_mask.shape, jnp.int32),
            vmem((width, pipes), F32),
            vmem((width, nodes), F32),
            vmem((width, nodes), F32),
            vmem((width, store), F32),
            vmem((width, pipes), F32),
            vmem((2 * width, pipes), BF16),
            vmem((2 * width, nodes), BF16),
            vmem((width, store), F32),
            vmem((nodes, all_slots + store), BF16),
            vmem((8, all_slots), F32),
            vmem((width, store), F32),
            vmem((n_msg, HALVES, half * all_slots // 128, 128), F32),
            vmem((n_msg, HALVES, half * all_slots // 128, 128), F32),
            vmem((ITERS, 2, 8, store), F32),
            vmem((ITERS, 2, 8, store), F32),
            sem((12,)),
            sem((8,)),
            sem((4,)),
            sem((3,)),
            sem((n_msg, HALVES, 2)),
            sem((n_msg, HALVES, 2)),
            sem((ITERS, 2)),
            sem((ITERS, 2)),
        ],
        compiler_params=pltpu.CompilerParams(
            collective_id=0, has_side_effects=True, vmem_limit_bytes=56 * 2**20
        ),
    )(*args)
    return pl.pallas_call(
        store_all,
        out_shape=tuple(jax.ShapeDtypeStruct(r.shape, r.dtype) for r in results),
        in_specs=[any_spec] * 3,
        out_specs=(any_spec,) * 3,
        scratch_shapes=[vmem(r.shape, F32) for r in results] + [sem((3,)), sem((3,))],
    )(*results)


def solution(mesh):
    placed = (
        P("dom", None),
        P("dom", None),
        P("dom", None, None),
        P(),
        P("dom", None),
        P("dom", None),
        P("dom", "hour"),
        P("dom", "hour"),
        P("dom", "hour"),
        P("dom", "hour"),
        P("dom"),
        P("dom"),
        P("dom"),
        P("dom"),
    )
    return jax.shard_map(
        body,
        mesh=mesh,
        in_specs=placed,
        out_specs=(P("dom", "hour"), P("dom", "hour"), P("dom", "hour")),
        check_vma=False,
    )
```

```python
import jax
import jax.numpy as jnp
from jax import lax
from jax.experimental import pallas as pl
from jax.experimental.pallas import tpu as pltpu
from jax.sharding import PartitionSpec as P

ITERS = 2
STEP = 0.3
HALVES = 2
MESH = pl.DeviceIdType.MESH
F32 = jnp.float32
BF16 = jnp.bfloat16
NN = (((1,), (0,)), ((), ()))
NT = (((1,), (1,)), ((), ()))

GROUPS = (
    ((4, 1), (4, 0), (3, 1), (3, 0), (-3, 1), (-3, 0), (0, 1), (0, 0)),
    ((2, 1), (2, 0), (-2, 1), (-2, 0), (1, 1), (1, 0), (-1, 1), (-1, 0)),
)
BLOCKS = GROUPS[0] + GROUPS[1]
PER = len(GROUPS[0])
OWN = BLOCKS.index((0, 0))
MIRROR = [BLOCKS.index((4 if dz == 4 else -dz, flip)) for dz, flip in BLOCKS]


def dot(a, b, dims):
    return lax.dot_general(a, b, dims, preferred_element_type=F32)


def parts(x):
    hi = x.astype(BF16)
    lo = (x - hi.astype(F32)).astype(BF16)
    return hi, lo


def product(hi, lo, mat_hi, mat_lo, dims):
    n = hi.shape[0]
    both = dot(jnp.concatenate([hi, lo], axis=0), mat_hi, dims)
    return both[:n] + both[n:] + dot(hi, mat_lo, dims)


def exact(hi, lo, onehot, dims):
    n = hi.shape[0]
    both = dot(jnp.concatenate([hi, lo], axis=0), onehot, dims)
    return both[:n] + both[n:]


def swap_blocks(blocks, slots):
    count = len(blocks)
    group = lax.broadcasted_iota(jnp.int32, blocks[0].shape, 1) // slots
    result = []
    for i in range(count):
        out = blocks[i]
        for j in range(count):
            if j != i:
                out = jnp.where(group == j, pltpu.roll(blocks[j], ((j - i) % count) * slots, 1), out)
        result.append(out)
    return result


def kernel(
    inc_local, inc_bound, bound_rows, bound_count, presence, stor_nodes,
    flow0, stor0, dual0, demand, pipe_cost, pipe_cap, stor_cost, stor_cap,
    flow_out, level_out, dual_out,
    loc32, bnd32, loc_hi, loc_lo, bnd_hi, bnd_lo, bt_hi, bt_lo,
    nat_f, nat_y, nat_d, nat_s, rows_v, stor_v, cost_v, cap_v, scost_v, scap_v, count_s, pres_s,
    f_t, y_t, d_t, s_t, g_t, fb, yb, sd, onehot, live, w_t,
    send, recv, halo_send, halo_recv,
    in_sem, loc_sem, bnd_sem, out_sem, send_sem, recv_sem, halo_send_sem, halo_recv_sem,
):
    me = lax.axis_index("dom")
    hour = lax.axis_index("hour")
    hours = lax.axis_size("hour")
    nodes, pipes = inc_local.shape
    slots = bound_rows.shape[1]
    store = stor_nodes.shape[1]
    width = flow0.shape[1]
    half = width // HALVES
    msg = half * slots // 128
    per_tile = 128 // slots
    cols = PER * slots
    all_slots = 2 * cols

    def dom_at(dz, flip):
        z, core = me // 2, lax.rem(me, 2)
        z = lax.rem(z + (dz + 8), 8)
        return z * 2 + (1 - core if flip else core)

    nxt = lax.rem(hour + 1, hours)
    prv = lax.rem(hour + hours - 1, hours)

    barrier = pltpu.get_barrier_semaphore()
    for j, (dz, flip) in enumerate(BLOCKS):
        if j != OWN:
            pl.semaphore_signal(barrier, inc=1, device_id={"dom": dom_at(dz, flip)}, device_id_type=MESH)
    pl.semaphore_signal(barrier, inc=1, device_id={"hour": nxt}, device_id_type=MESH)
    pl.semaphore_signal(barrier, inc=1, device_id={"hour": prv}, device_id_type=MESH)

    ins = [
        (dual0, nat_y), (bound_rows, rows_v), (stor_nodes, stor_v), (bound_count, count_s), (presence, pres_s),
        (pipe_cost, cost_v), (pipe_cap, cap_v), (stor_cost, scost_v), (stor_cap, scap_v), (stor0, nat_s),
        (flow0, nat_f), (demand, nat_d),
    ]
    in_copies = [pltpu.make_async_copy(a, b, in_sem.at[i]) for i, (a, b) in enumerate(ins)]
    (cp_y, cp_rows, cp_stor, cp_count, cp_pres, cp_cost, cp_cap, cp_scost, cp_scap, cp_s, cp_f, cp_d) = in_copies
    n_loc = loc_sem.shape[0]
    n_bnd = bnd_sem.shape[0]
    step_loc = nodes // n_loc
    step_bnd = inc_bound.shape[0] // n_bnd

    def loc_copy(i):
        s = pl.ds(pl.multiple_of(i * step_loc, step_loc), step_loc)
        return pltpu.make_async_copy(inc_local.at[s], loc32.at[s], loc_sem.at[i])

    def bnd_copy(i):
        s = pl.ds(pl.multiple_of(i * step_bnd, step_bnd), step_bnd)
        return pltpu.make_async_copy(inc_bound.at[s], bnd32.at[s], bnd_sem.at[i])

    for c in in_copies[:10]:
        c.start()
    for i in range(n_loc):
        loc_copy(i).start()
    cp_f.start()
    for i in range(n_bnd):
        bnd_copy(i).start()
    cp_d.start()

    zero = jnp.zeros((msg, 128), F32)
    for x in range(2 * ITERS):
        for h in range(HALVES):
            recv[x, h, OWN * msg : (OWN + 1) * msg, :] = zero

    cp_rows.wait()
    cp_stor.wait()
    node = lax.broadcasted_iota(jnp.int32, (nodes, 128), 0)
    for t in range(all_slots // 128):
        pieces = [rows_v[pl.ds(dom_at(*BLOCKS[t * per_tile + p]), 1), :] for p in range(per_tile)]
        row = jnp.concatenate(pieces, axis=1)
        onehot[:, t * 128 : (t + 1) * 128] = jnp.where(node == row, 1.0, 0.0).astype(BF16)
    onehot[:, all_slots:] = jnp.where(node == stor_v[...], 1.0, 0.0).astype(BF16)

    cp_count.wait()
    lane = lax.broadcasted_iota(jnp.int32, (8, 128), 1)
    for t in range(all_slots // 128):
        counts = jnp.zeros((8, 128), jnp.int32)
        for p in range(per_tile):
            counts = jnp.where(lane // slots == p, count_s[dom_at(*BLOCKS[t * per_tile + p]), me], counts)
        live[:, t * 128 : (t + 1) * 128] = jnp.where(lax.rem(lane, slots) < counts, 1.0, 0.0).astype(F32)

    cp_y.wait()
    for j in range(nodes // 128):
        s = slice(j * 128, (j + 1) * 128)
        y_t[:, s] = nat_y[s, :].T
    hi, lo = parts(y_t[...])
    yb[:width, :] = hi
    yb[width:, :] = lo

    def rows_of(h):
        return pl.ds(pl.multiple_of(h * half, half), half)

    def lows_of(h):
        return pl.ds(pl.multiple_of(width + h * half, half), half)

    def message(x, h, j):
        dz, flip = BLOCKS[j]
        k = MIRROR[j]
        return pltpu.make_async_remote_copy(
            src_ref=send.at[x, h, pl.ds(j * msg, msg)],
            dst_ref=recv.at[x, h, pl.ds(k * msg, msg)],
            send_sem=send_sem.at[x, h, j // PER],
            recv_sem=recv_sem.at[x, h, k // PER],
            device_id={"dom": dom_at(dz, flip)},
            device_id_type=MESH,
        )

    def whole(x, h, group):
        count = PER - 1 if OWN // PER == group else PER
        s = pl.ds(group * PER * msg, count * msg)
        return pltpu.make_async_remote_copy(
            src_ref=send.at[x, h, s],
            dst_ref=recv.at[x, h, s],
            send_sem=send_sem.at[x, h, group],
            recv_sem=recv_sem.at[x, h, group],
            device_id={"dom": dom_at(0, 1)},
            device_id_type=MESH,
        )

    def post(x, h, group, values):
        for t in range(cols // 128):
            blocks = [values[g * msg : (g + 1) * msg, t * 128 : (t + 1) * 128] for g in range(per_tile)]
            for p, out in enumerate(swap_blocks(blocks, slots)):
                j = group * PER + t * per_tile + p
                if j != OWN:
                    send[x, h, j * msg : (j + 1) * msg, :] = out
        for j in range(group * PER, (group + 1) * PER):
            if j != OWN:
                message(x, h, j).start()

    def fetch(x, h, group):
        whole(x, h, group).wait_recv()
        columns = []
        for t in range(cols // 128):
            first = group * PER + t * per_tile
            blocks = [recv[x, h, (first + p) * msg : (first + p + 1) * msg, :] for p in range(per_tile)]
            columns.append(jnp.concatenate(swap_blocks(blocks, slots), axis=0))
        return jnp.concatenate(columns, axis=1)

    def gather(it, h):
        values = exact(yb[rows_of(h), :], yb[lows_of(h), :], onehot[:, :all_slots], NN)
        for group in range(2):
            post(2 * it, h, group, values[:, group * cols : (group + 1) * cols])

    def scatter(it, h):
        hi, lo = parts(jnp.concatenate([fetch(2 * it + 1, h, group) for group in range(2)], axis=1))
        total = exact(hi, lo, onehot[:, :all_slots], NT)
        y = y_t[rows_of(h), :] - STEP * total
        y_t[rows_of(h), :] = y
        hi, lo = parts(y)
        yb[rows_of(h), :] = hi
        yb[lows_of(h), :] = lo

    def primal(it, h):
        r = rows_of(h)
        for group in range(2):
            s = slice(group * cols, (group + 1) * cols)
            hi, lo = parts(fetch(2 * it, h, group) * live[0:1, s])
            g_t[r, :] += product(hi, lo, bnd_hi[s, :], bnd_lo[s, :], NN)
        f = f_t[r, :]
        new = jnp.clip(f - STEP * (cost_v[...] - g_t[r, :]), 0.0, cap_v[...])
        f_t[r, :] = new
        hi, lo = parts(2.0 * new - f)
        fb[r, :] = hi
        fb[lows_of(h), :] = lo
        terms = product(fb[r, :], fb[lows_of(h), :], bt_hi[...], bt_lo[...], NN) * live[0:1, :]
        for group in range(2):
            s = slice(group * cols, (group + 1) * cols)
            post(2 * it + 1, h, group, terms[:, s])

    def halo(it, kind):
        return pltpu.make_async_remote_copy(
            src_ref=halo_send.at[it, kind],
            dst_ref=halo_recv.at[it, kind],
            send_sem=halo_send_sem.at[it, kind],
            recv_sem=halo_recv_sem.at[it, kind],
            device_id={"hour": nxt if kind else prv},
            device_id_type=MESH,
        )

    def prepare():
        cp_pres.wait()
        rows = 64
        bsize = pipes // presence.shape[1]

        def one_loc(i, _):
            @pl.when(lax.rem(i, step_loc // rows) == 0)
            def _():
                loc_copy(i // (step_loc // rows)).wait()

            s = pl.ds(pl.multiple_of(i * rows, rows), rows)
            for j in range(presence.shape[1]):
                c = slice(j * bsize, (j + 1) * bsize)
                scale = pres_s[i // (bsize // rows), j].astype(F32)
                hi, lo = parts(loc32[s, c] * scale)
                loc_hi[s, c] = hi
                loc_lo[s, c] = lo
            return 0

        lax.fori_loop(0, nodes // rows, one_loc, 0)
        g_t[...] = product(yb[:width, :], yb[width:, :], loc_hi[...], loc_lo[...], NN)

    def prepare_rest():
        cp_f.wait()
        for j in range(pipes // 128):
            s = slice(j * 128, (j + 1) * 128)
            f_t[:, s] = nat_f[s, :].T
        for i in range(n_bnd):
            bnd_copy(i).wait()
        for j, (dz, flip) in enumerate(BLOCKS):
            hi, lo = parts(bnd32[pl.ds(pl.multiple_of(dom_at(dz, flip) * slots, slots), slots), :])
            bnd_hi[j * slots : (j + 1) * slots, :] = hi
            bnd_lo[j * slots : (j + 1) * slots, :] = lo
        bt_hi[...] = bnd_hi[...].T
        bt_lo[...] = bnd_lo[...].T
        cp_d.wait()
        for j in range(nodes // 128):
            s = slice(j * 128, (j + 1) * 128)
            d_t[:, s] = nat_d[s, :].T
        cp_s.wait()
        s_t[...] = nat_s[...].T
        cp_cost.wait()
        cp_cap.wait()
        cp_scost.wait()
        cp_scap.wait()

    pl.semaphore_wait(barrier, PER * 2 - 1 + 2)

    row_of = lax.broadcasted_iota(jnp.int32, (width, store), 0)
    stor_cols = slice(all_slots, all_slots + store)

    def iteration(it, _):
        gather(it, 0)

        @pl.when(it > 0)
        def _():
            scatter(it - 1, 1)

        gather(it, 1)
        sd[...] = exact(yb[:width, :], yb[width:, :], onehot[:, stor_cols], NN)
        halo_send[it, 0] = sd[0:8, :]
        halo(it, 0).start()

        @pl.when(it == 0)
        def _():
            prepare()
            prepare_rest()

        @pl.when(it > 0)
        def _():
            g_t[...] = product(yb[:width, :], yb[width:, :], loc_hi[...], loc_lo[...], NN)

        halo(it, 0).wait_recv()
        now = sd[...]
        after = jnp.where(row_of == width - 1, halo_recv[it, 0, 0:1, :], pltpu.roll(now, width - 1, 0))
        s = s_t[...]
        new = jnp.clip(s - STEP * (scost_v[...] - (after - now)), 0.0, scap_v[...])
        s_t[...] = new
        bar = 2.0 * new - s
        w_t[...] = bar
        halo_send[it, 1] = bar[width - 8 :, :]
        halo(it, 1).start()

        primal(it, 0)
        primal(it, 1)

        halo(it, 1).wait_recv()
        bar = w_t[...]
        before = jnp.where(row_of == 0, halo_recv[it, 1, 7:8, :], pltpu.roll(bar, 1, 0))
        hi, lo = parts(before - bar)
        r = exact(hi, lo, onehot[:, stor_cols], NT)
        r = r + product(fb[:width, :], fb[width:, :], loc_hi[...], loc_lo[...], NT)
        y_t[...] = y_t[...] + STEP * (d_t[...] - r)
        scatter(it, 0)
        return 0

    lax.fori_loop(0, ITERS, iteration, 0)
    for j in range(pipes // 128):
        s = slice(j * 128, (j + 1) * 128)
        nat_f[s, :] = f_t[:, s].T
    nat_s[...] = s_t[...].T
    out_f = pltpu.make_async_copy(nat_f, flow_out, out_sem.at[0])
    out_f.start()
    out_s = pltpu.make_async_copy(nat_s, level_out, out_sem.at[1])
    out_s.start()
    scatter(ITERS - 1, 1)
    out_y = []
    for j in range(nodes // 128):
        s = slice(j * 128, (j + 1) * 128)
        nat_y[s, :] = y_t[:, s].T
        if j % 4 == 3:
            part = slice((j - 3) * 128, (j + 1) * 128)
            out_y.append(pltpu.make_async_copy(nat_y.at[part], dual_out.at[part], out_sem.at[2 + j // 4]))
            out_y[-1].start()
    for x in range(2 * ITERS):
        for h in range(HALVES):
            for group in range(2):
                whole(x, h, group).wait_send()
    for it in range(ITERS):
        for kind in range(2):
            halo(it, kind).wait_send()
    out_f.wait()
    out_s.wait()
    for c in out_y:
        c.wait()


def store_all(flow_in, level_in, dual_in, flow_out, level_out, dual_out, flow, level, dual, sems, in_sems):
    pieces = []
    for source, held, target in ((flow_in, flow, flow_out), (dual_in, dual, dual_out), (level_in, level, level_out)):
        rows = min(512, source.shape[0])
        for k in range(source.shape[0] // rows):
            pieces.append((source, held, target, pl.ds(k * rows, rows)))
    loads = [pltpu.make_async_copy(a.at[s], b.at[s], in_sems.at[i]) for i, (a, b, _, s) in enumerate(pieces)]
    stores = [pltpu.make_async_copy(b.at[s], c.at[s], sems.at[i]) for i, (_, b, c, s) in enumerate(pieces)]
    for c in loads:
        c.start()
    for a, c in zip(loads, stores):
        a.wait()
        c.start()
    for c in stores:
        c.wait()


def body(
    inc_local, inc_bound, bound_rows, bound_count, block_presence_mask, stor_nodes,
    flow0, stor0, dual0, demand, pipe_cost, pipe_cap, stor_cost, stor_cap,
):
    nodes, pipes = inc_local.shape
    store, width = stor0.shape
    peers, slots = bound_rows.shape[1:]
    all_slots = peers * slots
    half = width // HALVES
    n_msg = 2 * ITERS
    any_spec = pl.BlockSpec(memory_space=pl.ANY)
    vmem = pltpu.VMEM
    sem = pltpu.SemaphoreType.DMA
    args = (
        inc_local, inc_bound, bound_rows[0], bound_count, block_presence_mask, stor_nodes,
        flow0, stor0, dual0, demand, pipe_cost[None], pipe_cap[None], stor_cost[None], stor_cap[None],
    )
    results = pl.pallas_call(
        kernel,
        out_shape=(
            jax.ShapeDtypeStruct((pipes, width), F32),
            jax.ShapeDtypeStruct((store, width), F32),
            jax.ShapeDtypeStruct((nodes, width), F32),
        ),
        in_specs=[any_spec] * len(args),
        out_specs=(any_spec,) * 3,
        scratch_shapes=[
            vmem((nodes, pipes), F32),
            vmem((all_slots, pipes), F32),
            vmem((nodes, pipes), BF16),
            vmem((nodes, pipes), BF16),
            vmem((all_slots, pipes), BF16),
            vmem((all_slots, pipes), BF16),
            vmem((pipes, all_slots), BF16),
            vmem((pipes, all_slots), BF16),
            vmem((pipes, width), F32),
            vmem((nodes, width), F32),
            vmem((nodes, width), F32),
            vmem((store, width), F32),
            vmem((peers, slots), jnp.int32),
            vmem((1, store), jnp.int32),
            vmem((1, pipes), F32),
            vmem((1, pipes), F32),
            vmem((1, store), F32),
            vmem((1, store), F32),
            pltpu.SMEM(bound_count.shape, jnp.int32),
            pltpu.SMEM(block_presence_mask.shape, jnp.int32),
            vmem((width, pipes), F32),
            vmem((width, nodes), F32),
            vmem((width, nodes), F32),
            vmem((width, store), F32),
            vmem((width, pipes), F32),
            vmem((2 * width, pipes), BF16),
            vmem((2 * width, nodes), BF16),
            vmem((width, store), F32),
            vmem((nodes, all_slots + store), BF16),
            vmem((8, all_slots), F32),
            vmem((width, store), F32),
            vmem((n_msg, HALVES, half * all_slots // 128, 128), F32),
            vmem((n_msg, HALVES, half * all_slots // 128, 128), F32),
            vmem((ITERS, 2, 8, store), F32),
            vmem((ITERS, 2, 8, store), F32),
            sem((12,)),
            sem((8,)),
            sem((4,)),
            sem((2 + nodes // 512,)),
            sem((n_msg, HALVES, 2)),
            sem((n_msg, HALVES, 2)),
            sem((ITERS, 2)),
            sem((ITERS, 2)),
        ],
        compiler_params=pltpu.CompilerParams(
            collective_id=0, has_side_effects=True, vmem_limit_bytes=56 * 2**20
        ),
    )(*args)
    return pl.pallas_call(
        store_all,
        out_shape=tuple(jax.ShapeDtypeStruct(r.shape, r.dtype) for r in results),
        in_specs=[any_spec] * 3,
        out_specs=(any_spec,) * 3,
        scratch_shapes=[vmem(r.shape, F32) for r in results] + [sem((8,)), sem((8,))],
    )(*results)


def solution(mesh):
    placed = (
        P("dom", None),
        P("dom", None),
        P("dom", None, None),
        P(),
        P("dom", None),
        P("dom", None),
        P("dom", "hour"),
        P("dom", "hour"),
        P("dom", "hour"),
        P("dom", "hour"),
        P("dom"),
        P("dom"),
        P("dom"),
        P("dom"),
    )
    return jax.shard_map(
        body,
        mesh=mesh,
        in_specs=placed,
        out_specs=(P("dom", "hour"), P("dom", "hour"), P("dom", "hour")),
        check_vma=False,
    )
```
